32 devices in a mesh: grp: 4 (over z), pair: 8 (over y, x, core).
Axes of the slice: x: 2, y: 2, z: 4, core: 2. Of those that a mesh axis runs over, the one named last changes fastest.
Arguments:
- three_center: bfloat16 [512, 1024, 1024], P('pair', 'grp'), may hold values from -6 to 6
- virt_density: bfloat16 [1024, 1024], P(None, 'pair'), may hold values from -0.1875 to 0.1875
- occ_density: bfloat16 [1024, 1024], P(None, 'pair'), may hold values from -0.1875 to 0.1875
- tensor_mask: int32 [4, 8, 8], replicated, may hold values 0 or 1
- virt_mask: int32 [8, 8], replicated, may hold values 0 or 1
- occ_mask: int32 [8, 8], replicated, may hold values 0 or 1
- panel_order: int32 [512], replicated, may hold values from 0 to 511, each once
Outputs:
- response: float32 [512, 512], P(('grp', 'pair'))
The draws below stay inside these ranges and needn't reach their ends.
Inputs may be any that keep to these rules, and one draw needn't show every extreme that they name: `tensor_mask`: each block is 0 (absent) or 1 (present). `virt_mask`: each block is 0 (absent) or 1 (present). `occ_mask`: each block is 0 (absent) or 1 (present). `panel_order`: every auxiliary index appears exactly once.
All inputs are finite; a program needn't handle non-finite values.
Results may differ from the reference program's by a relative error of at most 0.0041.
Values may be sent and summed in bfloat16 or wider, within the bound.
A program may use at most 256 MiB of HBM per device.

```python
import jax
import jax.numpy as jnp
from jax import lax

NAUX = 512
NORB = 1024
BLK = 128


def plant(entries, stream_key, smallest, high):
    index_at = [jax.random.randint(jax.random.fold_in(stream_key, axis), (), 0, length) for axis, length in enumerate(entries.shape)]
    widest = entries.shape.index(max(entries.shape))
    next_to = index_at[:widest] + [(index_at[widest] + 1) % entries.shape[widest]] + index_at[widest + 1:]
    return entries.at[tuple(index_at)].set(smallest).at[tuple(next_to)].set(high)


def steps_of(rng, extent, cuts, least, high):
    def one(position, parts):
        draws = jax.random.uniform(jax.random.fold_in(jax.random.fold_in(rng, 6), position), (parts,), jnp.float32, least / len(cuts), high / len(cuts))
        return jnp.repeat(jnp.exp(draws), extent[position] // parts).reshape((-1,) + (1,) * (len(extent) - position - 1))

    gain = one(*cuts[0])
    for cut in cuts[1:]:
        gain = gain * one(*cut)
    return gain


def scatter_about(own_key, shape, deviation, limit, pieces=(), kind=jnp.bfloat16):
    entries = deviation * jax.random.normal(own_key, shape, jnp.float32)
    if pieces:
        entries = entries * steps_of(own_key, shape, pieces, -0.22, 0.18)
    return jnp.clip(entries, -limit, limit).astype(kind)


def setup_inputs(seed: int = 0) -> dict:
    arg_keys = jax.random.split(jax.random.key(seed), 8)
    return {
        "three_center": scatter_about(arg_keys[0], (NAUX, NORB, NORB), 1.0, 6.0, ((0, 8), (1, 4))),
        "virt_density": scatter_about(arg_keys[1], (NORB, NORB), NORB ** -0.5, 0.1875, ((1, 8),)),
        "occ_density": scatter_about(arg_keys[2], (NORB, NORB), NORB ** -0.5, 0.1875, ((1, 8),)),
        "tensor_mask": plant((jax.random.randint(arg_keys[3], (NAUX // BLK, NORB // BLK, NORB // BLK), 0, 4) < 3).astype(jnp.int32), jax.random.fold_in(arg_keys[3], 1), 0, 1),
        "virt_mask": plant((jax.random.randint(arg_keys[4], (NORB // BLK, NORB // BLK), 0, 4) < 3).astype(jnp.int32), jax.random.fold_in(arg_keys[4], 1), 0, 1),
        "occ_mask": plant((jax.random.randint(arg_keys[5], (NORB // BLK, NORB // BLK), 0, 4) < 3).astype(jnp.int32), jax.random.fold_in(arg_keys[5], 1), 0, 1),
        "panel_order": jax.random.permutation(arg_keys[6], NAUX).astype(jnp.int32),
    }


def spread_blocks(table):
    return jnp.repeat(jnp.repeat(table, BLK, axis=0), BLK, axis=1)


def reference(three_center, virt_density, occ_density, tensor_mask, virt_mask, occ_mask, panel_order):
    virt_live = virt_density * spread_blocks(virt_mask).astype(jnp.bfloat16)
    occ_live = occ_density * spread_blocks(occ_mask).astype(jnp.bfloat16)

    def one_block(block_id):
        rows = lax.dynamic_slice_in_dim(three_center, block_id * BLK, BLK, 0)
        table = lax.dynamic_index_in_dim(tensor_mask, block_id, 0, keepdims=False)
        masked = rows * spread_blocks(table).astype(jnp.bfloat16)[None]
        half = jnp.dot(masked.reshape(BLK * NORB, NORB), virt_live, preferred_element_type=jnp.float32)
        half = half.astype(jnp.bfloat16).reshape(BLK, NORB, NORB)
        turned = jnp.transpose(half, (0, 2, 1)).reshape(BLK * NORB, NORB)
        trans = jnp.dot(turned, occ_live, preferred_element_type=jnp.float32).astype(jnp.bfloat16)
        return masked.reshape(BLK, NORB * NORB), trans.reshape(BLK, NORB * NORB)

    block_ids = jnp.arange(NAUX // BLK, dtype=jnp.int32)
    masked_all, trans_all = lax.map(one_block, block_ids)
    masked_all = masked_all.reshape(NAUX, NORB * NORB)
    trans_all = trans_all.reshape(NAUX, NORB * NORB)
    picked = jnp.take(trans_all, panel_order.astype(jnp.int32), axis=0)
    product = lax.dot_general(picked, masked_all, (((1,), (1,)), ((), ())), preferred_element_type=jnp.float32)
    return product * (1.0 / NORB)
```

```python
import functools

import jax
import jax.numpy as jnp
from jax import lax
from jax.experimental import pallas as pl
from jax.experimental.pallas import tpu as pltpu
from jax.sharding import PartitionSpec as P

LANES = 128
MESH = pl.DeviceIdType.MESH
MIB = 1024 * 1024


def enter(grp, pair):
    g, p = lax.axis_index("grp"), lax.axis_index("pair")
    barrier = pltpu.get_barrier_semaphore()

    def greet(k, carry):
        there = lax.rem(g * pair + p + k, grp * pair)
        pl.semaphore_signal(
            barrier, inc=1, device_id=(there // pair, lax.rem(there, pair)), device_id_type=MESH
        )
        return carry

    lax.fori_loop(1, grp * pair, greet, 0)
    pl.semaphore_wait(barrier, grp * pair - 1)


def exchange_kernel(
    grp, pair, slots,
    tensor, virt_own, occ_own, mask,
    half_all, turn_all,
    tensor_buf, virt, occ, wide, half_buf, turn_buf,
    load_sem, half_send, turn_send, half_recv, turn_recv, dens_send, dens_recv,
):
    g, p = lax.axis_index("grp"), lax.axis_index("pair")
    slab, width, orbitals = tensor.shape
    chunk = tensor_buf.shape[1]
    chunks = slab // chunk
    rows = width // pair
    cols = virt_own.shape[0]
    blocks = mask.shape[1]
    edge = width // blocks
    steps = chunks * grp

    def load(c):
        return pltpu.make_async_copy(
            tensor.at[pl.ds(c * chunk, chunk)], tensor_buf.at[lax.rem(c, 2)],
            load_sem.at[lax.rem(c, 2)],
        )

    load(0).start()
    enter(grp, pair)

    def density(which, k):
        own, full = ((virt_own, virt), (occ_own, occ))[which]
        return pltpu.make_async_remote_copy(
            src_ref=own,
            dst_ref=full.at[pl.ds(pl.multiple_of(p * cols, cols), cols)],
            send_sem=dens_send.at[which, k],
            recv_sem=dens_recv.at[which, p],
            device_id=(g, lax.rem(p + k, pair)),
            device_id_type=MESH,
        )

    def density_arrived(which):
        full = (virt, occ)[which]
        for k in range(1, pair):
            sender = lax.rem(p + k, pair)
            part = full.at[pl.ds(pl.multiple_of(sender * cols, cols), cols)]
            pltpu.make_async_remote_copy(
                src_ref=part, dst_ref=part, send_sem=dens_send.at[which, k],
                recv_sem=dens_recv.at[which, sender],
                device_id=(g, sender), device_id_type=MESH,
            ).wait_recv()

    for which in range(2):
        for k in range(1, pair):
            density(which, k).start()
    own_rows = pl.ds(pl.multiple_of(p * cols, cols), cols)
    virt[own_rows, :] = virt_own[...]
    occ[own_rows, :] = occ_own[...]
    density_arrived(0)

    def place(buf, slot):
        def one(s, carry):
            for t in range(width // LANES):
                picked = wide[t, pl.ds(s, chunk, stride=width), :]
                buf[slot, s, :, t * LANES:(t + 1) * LANES] = picked.astype(buf.dtype)
            return carry

        lax.fori_loop(0, width, one, 0, unroll=8)

    def keep(i, product):
        for t in range(width // LANES):
            wide[t, pl.ds(pl.multiple_of(i * width, width), width), :] = (
                product[:, t * LANES:(t + 1) * LANES]
            )

    def wait_sent(buf, sems, slot):
        for k in range(pair):
            part = buf.at[slot, pl.ds(0, rows)]
            pltpu.make_async_copy(part, part, sems.at[slot, k]).wait()

    def send(buf, sends, slot, k, target_grp, dst, recv):
        target = lax.rem(p + k, pair)
        return pltpu.make_async_remote_copy(
            src_ref=buf.at[slot, pl.ds(target * rows, rows)], dst_ref=dst,
            send_sem=sends.at[slot, k], recv_sem=recv,
            device_id=(target_grp, target), device_id_type=MESH,
        )

    def stay(buf, sends, slot, dst):
        return pltpu.make_async_copy(
            buf.at[slot, pl.ds(p * rows, rows)], dst, sends.at[slot, 0]
        )

    def step(t, carry):
        c, u = t // grp, lax.rem(t, grp)
        b = lax.rem(c, 2)
        slot = lax.rem(t, slots)

        @pl.when(u == 0)
        def _():
            load(c).wait()

            @pl.when(c + 1 < chunks)
            def _():
                load(c + 1).start()

            def apply(i, carry):
                for block in range(blocks):
                    row = mask[c * chunk + i, block:block + 1, :]
                    row = jnp.broadcast_to(row, (16, orbitals)).astype(tensor_buf.dtype)
                    at = slice(block * edge, (block + 1) * edge)
                    part = tensor_buf[b, i, at, :].reshape(edge // 16, 16, orbitals)
                    tensor_buf[b, i, at, :] = (part * row[None]).reshape(edge, orbitals)
                return carry

            lax.fori_loop(0, chunk, apply, 0)

        @pl.when(t >= slots)
        def _():
            wait_sent(half_buf, half_send, slot)

        target_grp = lax.rem(g + 1 + u, grp)
        aux_rows = pl.ds(pl.multiple_of(p * slab + c * chunk, chunk), chunk)

        def half_one(i, carry):
            left = virt[pl.ds(pl.multiple_of(target_grp * width, width), width), :]
            keep(i, lax.dot_general(
                left, tensor_buf[b, i], (((1,), (1,)), ((), ())),
                preferred_element_type=jnp.float32,
            ))
            return carry

        lax.fori_loop(0, chunk, half_one, 0)
        place(half_buf, slot)
        dst = half_all.at[:, aux_rows, pl.ds(pl.multiple_of(g * width, width), width)]
        recv = half_recv.at[g * pair + p]

        @pl.when(target_grp == g)
        def _():
            stay(half_buf, half_send, slot, dst).start()

        @pl.when(target_grp != g)
        def _():
            send(half_buf, half_send, slot, 0, target_grp, dst, recv).start()

        for k in range(1, pair):
            send(half_buf, half_send, slot, k, target_grp, dst, recv).start()

        @pl.when(t == 0)
        def _():
            density_arrived(1)

        @pl.when(t >= slots)
        def _():
            wait_sent(turn_buf, turn_send, slot)

        section = pl.ds(pl.multiple_of(u * width, width), width)

        def turn_one(i, carry):
            keep(i, jnp.dot(
                tensor_buf[b, i], occ[:, section], preferred_element_type=jnp.float32
            ))
            return carry

        lax.fori_loop(0, chunk, turn_one, 0)
        place(turn_buf, slot)
        dst = turn_all.at[:, aux_rows, section]
        stay(turn_buf, turn_send, slot, dst).start()
        for k in range(1, pair):
            send(turn_buf, turn_send, slot, k, g, dst, turn_recv.at[p]).start()
        return carry

    lax.fori_loop(0, steps, step, 0)

    for t in range(max(steps - slots, 0), steps):
        wait_sent(half_buf, half_send, t % slots)
        wait_sent(turn_buf, turn_send, t % slots)
    for which in range(2):
        for k in range(1, pair):
            density(which, k).wait_send()

    def half_arrived(k, carry):
        sender = lax.rem(g * pair + p + k, grp * pair)
        sender_grp, sender_pair = sender // pair, lax.rem(sender, pair)
        part = half_all.at[
            :, pl.ds(pl.multiple_of(sender_pair * slab, slab), slab),
            pl.ds(pl.multiple_of(sender_grp * width, width), width),
        ]
        pltpu.make_async_remote_copy(
            src_ref=part, dst_ref=part, send_sem=half_send.at[0, 0],
            recv_sem=half_recv.at[sender],
            device_id=(sender_grp, sender_pair), device_id_type=MESH,
        ).wait_recv()
        return carry

    lax.fori_loop(1, grp * pair, half_arrived, 0)

    def turn_arrived(k, carry):
        sender = lax.rem(p + k, pair)
        part = turn_all.at[:, pl.ds(pl.multiple_of(sender * slab, slab), slab), :]
        pltpu.make_async_remote_copy(
            src_ref=part, dst_ref=part, send_sem=turn_send.at[0, 0],
            recv_sem=turn_recv.at[sender],
            device_id=(g, sender), device_id_type=MESH,
        ).wait_recv()
        return carry

    lax.fori_loop(1, pair, turn_arrived, 0)


def exchange(grp, pair, tensor, virt_own, occ_own, mask):
    slab, width, orbitals = tensor.shape
    chunk = 16
    slots = min(4, slab // chunk * grp)
    gathered = jax.ShapeDtypeStruct((width // pair, slab * pair, orbitals), tensor.dtype)
    flops = 4 * slab * width * orbitals * orbitals
    return pl.pallas_call(
        functools.partial(exchange_kernel, grp, pair, slots),
        out_shape=(gathered, gathered),
        in_specs=[pl.BlockSpec(memory_space=pl.ANY)]
        + [pl.BlockSpec(memory_space=pltpu.VMEM)] * 3,
        out_specs=(pl.BlockSpec(memory_space=pl.ANY),) * 2,
        scratch_shapes=[
            pltpu.VMEM((2, chunk, width, orbitals), tensor.dtype),
            pltpu.VMEM((orbitals, orbitals), tensor.dtype),
            pltpu.VMEM((orbitals, orbitals), tensor.dtype),
            pltpu.VMEM((width // LANES, chunk * width, LANES), jnp.float32),
            pltpu.VMEM((slots, width, chunk, width), tensor.dtype),
            pltpu.VMEM((slots, width, chunk, width), tensor.dtype),
            pltpu.SemaphoreType.DMA((2,)),
            pltpu.SemaphoreType.DMA((slots, pair)),
            pltpu.SemaphoreType.DMA((slots, pair)),
            pltpu.SemaphoreType.DMA((grp * pair,)),
            pltpu.SemaphoreType.DMA((pair,)),
            pltpu.SemaphoreType.DMA((2, pair)),
            pltpu.SemaphoreType.DMA((2, pair)),
        ],
        compiler_params=pltpu.CompilerParams(
            collective_id=0, has_side_effects=True, vmem_limit_bytes=56 * MIB
        ),
        cost_estimate=pl.CostEstimate(
            flops=flops, bytes_accessed=6 * slab * width * orbitals, transcendentals=0
        ),
    )(tensor, virt_own, occ_own, mask)


def product_kernel(scale, order, half, turn, out, total):
    s = pl.program_id(0)

    @pl.when(s == 0)
    def _():
        total[...] = jnp.zeros_like(total)

    total[...] += lax.dot_general(
        half[...], turn[...], (((1,), (1,)), ((), ())), preferred_element_type=jnp.float32
    )

    @pl.when(s == pl.num_programs(0) - 1)
    def _():
        share = out.shape[1]

        def device(d, carry):
            for r in range(share):
                out[d, r:r + 1, :] = total[pl.ds(order[d * share + r], 1), :] * scale
            return carry

        lax.fori_loop(0, out.shape[0], device, 0)


def product(devices, half_all, turn_all, order):
    rows, aux, orbitals = half_all.shape
    block = pl.BlockSpec((None, aux, orbitals), lambda s: (s, 0, 0))
    out = (devices, aux // devices, aux)
    return pl.pallas_call(
        functools.partial(product_kernel, 1.0 / orbitals),
        grid=(rows,),
        out_shape=jax.ShapeDtypeStruct(out, jnp.float32),
        in_specs=[pl.BlockSpec(memory_space=pltpu.SMEM), block, block],
        out_specs=pl.BlockSpec(out, lambda s: (0, 0, 0)),
        scratch_shapes=[pltpu.VMEM((aux, aux), jnp.float32)],
        compiler_params=pltpu.CompilerParams(vmem_limit_bytes=32 * MIB),
        cost_estimate=pl.CostEstimate(
            flops=2 * rows * aux * aux * orbitals,
            bytes_accessed=4 * rows * aux * orbitals, transcendentals=0,
        ),
    )(order, half_all, turn_all)


def sum_kernel(grp, pair, partial, out, arrived, send_sem, recv_sem):
    g, p = lax.axis_index("grp"), lax.axis_index("pair")
    devices = grp * pair
    me = g * pair + p
    enter(grp, pair)

    def copy(k):
        there = lax.rem(me + k, devices)
        return pltpu.make_async_remote_copy(
            src_ref=partial.at[there], dst_ref=arrived.at[me],
            send_sem=send_sem.at[k], recv_sem=recv_sem.at[me],
            device_id=(there // pair, lax.rem(there, pair)), device_id_type=MESH,
        )

    def start(k, carry):
        copy(k).start()
        return carry

    lax.fori_loop(1, devices, start, 0)
    out[...] = partial[me]

    def add(k, carry):
        sender = lax.rem(me + devices - k, devices)
        pltpu.make_async_remote_copy(
            src_ref=partial.at[sender], dst_ref=arrived.at[sender],
            send_sem=send_sem.at[k], recv_sem=recv_sem.at[sender],
            device_id=(sender // pair, lax.rem(sender, pair)), device_id_type=MESH,
        ).wait_recv()
        out[...] += arrived[sender]
        return carry

    lax.fori_loop(1, devices, add, 0)

    def sent(k, carry):
        copy(k).wait_send()
        return carry

    lax.fori_loop(1, devices, sent, 0)


def sum_shares(grp, pair, partial):
    devices, share, aux = partial.shape
    return pl.pallas_call(
        functools.partial(sum_kernel, grp, pair),
        out_shape=jax.ShapeDtypeStruct((share, aux), jnp.float32),
        in_specs=[pl.BlockSpec(memory_space=pltpu.VMEM)],
        out_specs=pl.BlockSpec(memory_space=pltpu.VMEM),
        scratch_shapes=[
            pltpu.VMEM((devices, share, aux), jnp.float32),
            pltpu.SemaphoreType.DMA((devices,)),
            pltpu.SemaphoreType.DMA((devices,)),
        ],
        compiler_params=pltpu.CompilerParams(
            collective_id=1, has_side_effects=True, vmem_limit_bytes=16 * MIB
        ),
    )(partial)


def density_own(density, mask_table, first):
    orbitals, cols = density.shape
    edge = orbitals // mask_table.shape[0]
    of = (first + jnp.arange(cols, dtype=jnp.int32)) // edge
    table = jnp.take(mask_table.T, of, axis=0).astype(density.dtype)
    return density.T * jnp.repeat(table, edge, axis=1)


def per_device(
    grp, pair,
    three_center, virt_density, occ_density, tensor_mask, virt_mask, occ_mask, panel_order,
):
    slab, width, orbitals = three_center.shape
    g, p = lax.axis_index("grp"), lax.axis_index("pair")
    cols = virt_density.shape[1]
    edge = orbitals // tensor_mask.shape[1]
    virt_own = density_own(virt_density, virt_mask, p * cols)
    occ_own = density_own(occ_density, occ_mask, p * cols)
    of = (p * slab + jnp.arange(slab, dtype=jnp.int32)) // edge
    table = lax.dynamic_slice_in_dim(tensor_mask, g * width // edge, width // edge, 1)
    mask = jnp.repeat(jnp.take(table, of, axis=0).astype(jnp.float32), edge, axis=2)
    half_all, turn_all = exchange(grp, pair, three_center, virt_own, occ_own, mask)
    partial = product(grp * pair, half_all, turn_all, panel_order)
    return sum_shares(grp, pair, partial)


def solution(mesh):
    placed = (P("pair", "grp", None), P(None, "pair"), P(None, "pair"), P(), P(), P(), P())
    sizes = mesh.shape["grp"], mesh.shape["pair"]
    return jax.shard_map(
        functools.partial(per_device, *sizes),
        mesh=mesh, in_specs=placed, out_specs=P(("grp", "pair"), None), check_vma=False,
    )
```

```python
import functools

import jax
import jax.numpy as jnp
from jax import lax
from jax.experimental import pallas as pl
from jax.experimental.pallas import tpu as pltpu
from jax.sharding import PartitionSpec as P

LANES = 128
MESH = pl.DeviceIdType.MESH
MIB = 1024 * 1024


def enter(grp, pair):
    g, p = lax.axis_index("grp"), lax.axis_index("pair")
    barrier = pltpu.get_barrier_semaphore()

    def greet(k, carry):
        there = lax.rem(g * pair + p + k, grp * pair)
        pl.semaphore_signal(
            barrier, inc=1, device_id=(there // pair, lax.rem(there, pair)), device_id_type=MESH
        )
        return carry

    lax.fori_loop(1, grp * pair, greet, 0)
    pl.semaphore_wait(barrier, grp * pair - 1)


def response_kernel(
    grp, pair, half_slots, turn_slots,
    tensor, virt_own, occ_own, mask, order,
    half_all, turn_all, out,
    tensor_buf, virt, occ, wide, half_buf, turn_buf, total, shares, arrived, column, crossed,
    load_sem, half_send, turn_send, half_recv, turn_recv, dens_send, dens_recv,
    share_send, share_recv, cross_send, cross_recv,
):
    g, p = lax.axis_index("grp"), lax.axis_index("pair")
    slab, width, orbitals = tensor.shape
    chunk = tensor_buf.shape[1]
    chunks = slab // chunk
    rows = width // pair
    cols = virt_own.shape[0]
    blocks = mask.shape[1]
    edge = width // blocks
    parts = width // LANES
    steps = parts * chunks * grp
    sibling = p + 1 - 2 * lax.rem(p, 2)

    def load(c):
        return pltpu.make_async_copy(
            tensor.at[pl.ds(lax.rem(c, chunks) * chunk, chunk)], tensor_buf.at[lax.rem(c, 2)],
            load_sem.at[lax.rem(c, 2)],
        )

    load(0).start()
    enter(grp, pair)

    def remote(src, dst, send_sem, recv_sem, to_grp, to_pair):
        return pltpu.make_async_remote_copy(
            src_ref=src, dst_ref=dst, send_sem=send_sem, recv_sem=recv_sem,
            device_id=(to_grp, to_pair), device_id_type=MESH,
        )

    def slab_of(which, q):
        return (virt, occ)[which].at[pl.ds(pl.multiple_of(q * cols, cols), cols)]

    def density(which, k):
        to = sibling if k == 0 else lax.rem(p + 2 * k, pair)
        return remote(
            (virt_own, occ_own)[which], slab_of(which, p),
            dens_send.at[which, k], dens_recv.at[which, p], g, to,
        )

    def density_in(which, q):
        part = slab_of(which, q)
        remote(part, part, dens_send.at[which, 0], dens_recv.at[which, q], g, sibling).wait_recv()

    def density_on(which, k):
        q = lax.rem(p + 2 * k, pair)
        part = slab_of(which, q)
        return remote(
            part, part, dens_send.at[which, pair // 2 + k], dens_recv.at[which, q], g, sibling
        )

    def pass_on(which):
        for k in range(1, pair // 2):
            density_in(which, lax.rem(p + 2 * k, pair))
            density_on(which, k).start()

    def rest_in(which):
        for k in range(pair // 2):
            density_in(which, lax.rem(sibling + 2 * k, pair))

    own_rows = pl.ds(pl.multiple_of(p * cols, cols), cols)
    for k in range(pair // 2):
        density(0, k).start()
    virt[own_rows, :] = virt_own[...]
    occ[own_rows, :] = occ_own[...]
    pass_on(0)
    for k in range(pair // 2):
        density(1, k).start()
    rest_in(0)

    def place(buf, slot):
        def one(s, carry):
            buf[slot, s] = wide[pl.ds(s, chunk, stride=width), :].astype(buf.dtype)
            return carry

        lax.fori_loop(0, width, one, 0, unroll=8)

    def keep(i, product):
        wide[pl.ds(pl.multiple_of(i * width, width), width), :] = product

    def wait_sent(buf, sems, slot):
        for k in range(pair):
            part = buf.at[slot, pl.ds(0, rows)]
            pltpu.make_async_copy(part, part, sems.at[slot, k]).wait()

    def send(buf, sends, slot, k, target_grp, dst, recv):
        target = lax.rem(p + k, pair)
        return remote(
            buf.at[slot, pl.ds(target * rows, rows)], dst, sends.at[slot, k], recv,
            target_grp, target,
        )

    def stay(buf, sends, slot, dst):
        return pltpu.make_async_copy(
            buf.at[slot, pl.ds(p * rows, rows)], dst, sends.at[slot, 0]
        )

    def step(t, carry):
        n, u = t // grp, lax.rem(t, grp)
        j, c = n // chunks, lax.rem(n, chunks)
        b = lax.rem(n, 2)
        half_slot, turn_slot = lax.rem(t, half_slots), lax.rem(t, turn_slots)

        @pl.when(u == 0)
        def _():
            load(n).wait()

            @pl.when(n + 1 < parts * chunks)
            def _():
                load(n + 1).start()

            def apply(i, carry):
                for block in range(blocks):
                    row = mask[c * chunk + i, block:block + 1, :]
                    row = jnp.broadcast_to(row, (16, orbitals)).astype(tensor_buf.dtype)
                    at = slice(block * edge, (block + 1) * edge)
                    part = tensor_buf[b, i, at, :].reshape(edge // 16, 16, orbitals)
                    tensor_buf[b, i, at, :] = (part * row[None]).reshape(edge, orbitals)
                return carry

            lax.fori_loop(0, chunk, apply, 0)

        @pl.when(t >= half_slots)
        def _():
            wait_sent(half_buf, half_send, half_slot)

        target_grp = lax.rem(g + 1 + u, grp)
        aux_rows = pl.ds(pl.multiple_of(p * slab + c * chunk, chunk), chunk)
        section = pl.ds(pl.multiple_of(j * LANES, LANES), LANES)

        def half_one(i, carry):
            left = virt[pl.ds(pl.multiple_of(target_grp * width, width), width), :]
            keep(i, lax.dot_general(
                left, tensor_buf[b, i, section, :], (((1,), (1,)), ((), ())),
                preferred_element_type=jnp.float32,
            ))
            return carry

        lax.fori_loop(0, chunk, half_one, 0)
        place(half_buf, half_slot)
        dst = half_all.at[j, :, aux_rows, pl.ds(pl.multiple_of(g * LANES, LANES), LANES)]
        recv = half_recv.at[j, g * pair + p]

        @pl.when(target_grp == g)
        def _():
            stay(half_buf, half_send, half_slot, dst).start()

        @pl.when(target_grp != g)
        def _():
            send(half_buf, half_send, half_slot, 0, target_grp, dst, recv).start()

        for k in range(1, pair):
            send(half_buf, half_send, half_slot, k, target_grp, dst, recv).start()

        @pl.when(t == 0)
        def _():
            pass_on(1)
            rest_in(1)

        @pl.when(t >= turn_slots)
        def _():
            wait_sent(turn_buf, turn_send, turn_slot)

        columns = pl.ds(pl.multiple_of(u * width + j * LANES, LANES), LANES)

        def turn_one(i, carry):
            keep(i, jnp.dot(
                tensor_buf[b, i], occ[:, columns], preferred_element_type=jnp.float32
            ))
            return carry

        lax.fori_loop(0, chunk, turn_one, 0)
        place(turn_buf, turn_slot)
        dst = turn_all.at[j, :, aux_rows, pl.ds(pl.multiple_of(u * LANES, LANES), LANES)]
        stay(turn_buf, turn_send, turn_slot, dst).start()
        for k in range(1, pair):
            send(turn_buf, turn_send, turn_slot, k, g, dst, turn_recv.at[j, p]).start()
        return carry

    lax.fori_loop(0, steps, step, 0)

    def all_in(j):
        def half_in(k, carry):
            sender = lax.rem(g * pair + p + k, grp * pair)
            sender_grp, sender_pair = sender // pair, lax.rem(sender, pair)
            part = half_all.at[
                j, :, pl.ds(pl.multiple_of(sender_pair * slab, slab), slab),
                pl.ds(pl.multiple_of(sender_grp * LANES, LANES), LANES),
            ]
            remote(
                part, part, half_send.at[0, 0], half_recv.at[j, sender], sender_grp, sender_pair
            ).wait_recv()
            return carry

        lax.fori_loop(1, grp * pair, half_in, 0)

        def turn_in(k, carry):
            sender = lax.rem(p + k, pair)
            part = turn_all.at[j, :, pl.ds(pl.multiple_of(sender * slab, slab), slab), :]
            remote(
                part, part, turn_send.at[0, 0], turn_recv.at[j, sender], g, sender
            ).wait_recv()
            return carry

        lax.fori_loop(1, pair, turn_in, 0)

    group = 4 if rows % 4 == 0 else 1
    aux = total.shape[0]

    def add_product(half, turn):
        value = total[...]
        for s in range(group):
            value += lax.dot_general(
                half[s], turn[s], (((1,), (1,)), ((), ())), preferred_element_type=jnp.float32
            )
        total[...] = value

    block = pl.BlockSpec((group, aux, grp * LANES), lambda s: (s, 0, 0))
    multiply = pltpu.emit_pipeline(add_product, grid=(rows // group,), in_specs=[block, block])

    total[...] = jnp.zeros_like(total)
    for j in range(parts):
        if j == parts - 1:
            for t in range(max(steps - half_slots, 0), steps):
                wait_sent(half_buf, half_send, t % half_slots)
            for t in range(max(steps - turn_slots, 0), steps):
                wait_sent(turn_buf, turn_send, t % turn_slots)
        all_in(j)
        multiply(half_all.at[j], turn_all.at[j])

    share = out.shape[0]

    def pick(d, carry):
        for r in range(share):
            row = total[pl.ds(order[d * share + r], 1), :]
            shares[lax.rem(d, pair), d // pair, r:r + 1, :] = row * (1.0 / orbitals)
        return carry

    lax.fori_loop(0, grp * pair, pick, 0)

    def over_pair(k):
        to = lax.rem(p + k, pair)
        return remote(shares.at[to], arrived.at[p], share_send.at[k], share_recv.at[p], g, to)

    for k in range(1, pair):
        over_pair(k).start()
    column[...] = shares[p]
    for k in range(1, pair):
        sender = lax.rem(p + pair - k, pair)
        part = arrived.at[sender]
        remote(part, part, share_send.at[k], share_recv.at[sender], g, sender).wait_recv()
        column[...] += arrived[sender]

    def over_grp(k):
        to = lax.rem(g + k, grp)
        return remote(column.at[to], crossed.at[g], cross_send.at[k], cross_recv.at[g], to, p)

    for k in range(1, grp):
        over_grp(k).start()
    out[...] = column[g]
    for k in range(1, grp):
        sender = lax.rem(g + grp - k, grp)
        part = crossed.at[sender]
        remote(part, part, cross_send.at[k], cross_recv.at[sender], sender, p).wait_recv()
        out[...] += crossed[sender]

    for k in range(1, grp):
        over_grp(k).wait_send()
    for k in range(1, pair):
        over_pair(k).wait_send()
    for which in range(2):
        for k in range(pair // 2):
            density(which, k).wait_send()
        for k in range(1, pair // 2):
            density_on(which, k).wait_send()


def response_share(grp, pair, tensor, virt_own, occ_own, mask, order):
    slab, width, orbitals = tensor.shape
    chunk = 16
    parts = width // LANES
    aux = slab * pair
    share = aux // (grp * pair)
    steps = parts * slab // chunk * grp
    half_slots, turn_slots = min(14, steps), min(8, steps)
    gathered = jax.ShapeDtypeStruct((parts, width // pair, aux, grp * LANES), tensor.dtype)
    kept = pltpu.VMEM
    dma = pltpu.SemaphoreType.DMA
    return pl.pallas_call(
        functools.partial(response_kernel, grp, pair, half_slots, turn_slots),
        out_shape=(gathered, gathered, jax.ShapeDtypeStruct((share, aux), jnp.float32)),
        in_specs=[pl.BlockSpec(memory_space=pl.ANY)]
        + [pl.BlockSpec(memory_space=kept)] * 3
        + [pl.BlockSpec(memory_space=pltpu.SMEM)],
        out_specs=(pl.BlockSpec(memory_space=pl.ANY),) * 2 + (pl.BlockSpec(memory_space=kept),),
        scratch_shapes=[
            kept((2, chunk, width, orbitals), tensor.dtype),
            kept((orbitals, orbitals), tensor.dtype),
            kept((orbitals, orbitals), tensor.dtype),
            kept((chunk * width, LANES), jnp.float32),
            kept((half_slots, width, chunk, LANES), tensor.dtype),
            kept((turn_slots, width, chunk, LANES), tensor.dtype),
            kept((aux, aux), jnp.float32),
            kept((pair, grp, share, aux), jnp.float32),
            kept((pair, grp, share, aux), jnp.float32),
            kept((grp, share, aux), jnp.float32),
            kept((grp, share, aux), jnp.float32),
            dma((2,)),
            dma((half_slots, pair)),
            dma((turn_slots, pair)),
            dma((parts, grp * pair)),
            dma((parts, pair)),
            dma((2, pair)),
            dma((2, pair)),
            dma((pair,)),
            dma((pair,)),
            dma((grp,)),
            dma((grp,)),
        ],
        compiler_params=pltpu.CompilerParams(
            collective_id=0, has_side_effects=True, vmem_limit_bytes=62 * MIB
        ),
        cost_estimate=pl.CostEstimate(
            flops=5 * slab * width * orbitals * orbitals,
            bytes_accessed=12 * slab * width * orbitals, transcendentals=0,
        ),
    )(tensor, virt_own, occ_own, mask, order)[2]


def density_own(density, mask_table, first):
    orbitals, cols = density.shape
    edge = orbitals // mask_table.shape[0]
    of = (first + jnp.arange(cols, dtype=jnp.int32)) // edge
    table = jnp.take(mask_table.T, of, axis=0).astype(density.dtype)
    return density.T * jnp.repeat(table, edge, axis=1)


def per_device(
    grp, pair,
    three_center, virt_density, occ_density, tensor_mask, virt_mask, occ_mask, panel_order,
):
    slab, width, orbitals = three_center.shape
    g, p = lax.axis_index("grp"), lax.axis_index("pair")
    cols = virt_density.shape[1]
    edge = orbitals // tensor_mask.shape[1]
    virt_own = density_own(virt_density, virt_mask, p * cols)
    occ_own = density_own(occ_density, occ_mask, p * cols)
    of = (p * slab + jnp.arange(slab, dtype=jnp.int32)) // edge
    table = lax.dynamic_slice_in_dim(tensor_mask, g * width // edge, width // edge, 1)
    mask = jnp.repeat(jnp.take(table, of, axis=0).astype(jnp.float32), edge, axis=2)
    return response_share(grp, pair, three_center, virt_own, occ_own, mask, panel_order)


def solution(mesh):
    placed = (P("pair", "grp", None), P(None, "pair"), P(None, "pair"), P(), P(), P(), P())
    sizes = mesh.shape["grp"], mesh.shape["pair"]
    return jax.shard_map(
        functools.partial(per_device, *sizes),
        mesh=mesh, in_specs=placed, out_specs=P(("grp", "pair"), None), check_vma=False,
    )
```
